32 devices in a mesh: fold: 8 (over z, x), blk: 4 (over y, core).
Axes of the slice: x: 2, y: 2, z: 4, core: 2. Of those that a mesh axis runs over, the one named last changes fastest.
Arguments:
- genotypes: bfloat16 [65536, 4096], P('fold', 'blk'), may hold values from 0 to 2, as said below
- phenotypes: bfloat16 [32, 65536], P(None, 'fold'), may hold values from -4 to 4
- trait_order: int32 [32], replicated, may hold values from 0 to 31, each once
Outputs:
- predict: float32 [32, 65536], P('blk', 'fold')
The draws below stay inside these ranges and needn't reach their ends.
Inputs may be any that keep to these rules, and one draw needn't show every extreme that they name: `genotypes`: dosages are 0, 1 or 2. `trait_order`: a permutation of the 32 traits.
All inputs are finite; a program needn't handle non-finite values.
Results may differ from the reference program's by a relative error of at most 0.00235.
Values may be sent and summed in bfloat16 or wider, within the bound.
A program may use at most 320 MiB of HBM per device.

```python
import jax
import jax.numpy as jnp
from jax import lax

S_DEV = 8192
B = 512
P_SIZE = 32
R = 2
ITERS = 8
SEG = 32
NB = 8
NVAR = 4096
NSAMP = 65536
Q = 16
N_FOLD = 8


def segment_bits(key, segment, fold_of):
    seg_key = jax.random.fold_in(key, segment)
    permille = jax.random.randint(jax.random.fold_in(seg_key, 0), (), 50, 301)
    fold_total = NSAMP // S_DEV
    allele_freq = permille * (fold_total - 1 + 2 * fold_of) // (2 * (fold_total - 1))
    ancestor = (jax.random.randint(jax.random.fold_in(seg_key, 1), (2, NSAMP), 0, 1000) < allele_freq[None, :]).astype(jnp.int32)
    copied = jax.random.randint(jax.random.fold_in(seg_key, 2), (2, NSAMP, SEG), 0, 1000) < 700
    fresh_bits = (jax.random.randint(jax.random.fold_in(seg_key, 3), (2, NSAMP, SEG), 0, 1000) < allele_freq[None, :, None]).astype(jnp.int32)
    hap_bits = jnp.where(copied, ancestor[:, :, None], fresh_bits)
    return (ancestor, hap_bits, allele_freq)


def draw_genotypes(key, part):
    fold_of = jnp.arange(NSAMP, dtype=jnp.int32) // S_DEV

    def per_segment(segment):
        ancestor, hap_bits, allele_freq = segment_bits(key, segment, fold_of)
        return (hap_bits[0] + hap_bits[1]).astype(jnp.float32).astype(jnp.bfloat16)
    pieces = lax.map(per_segment, jnp.arange(NVAR // SEG, dtype=jnp.int32))
    return jnp.transpose(pieces, (1, 0, 2)).reshape(NSAMP, NVAR)


def draw_phenotypes(key, part):
    fold_of = jnp.arange(NSAMP, dtype=jnp.int32) // S_DEV
    seg_total = NVAR // SEG

    def per_segment(segment):
        ancestor, hap_bits, allele_freq = segment_bits(key, segment, fold_of)
        return (ancestor[0] + ancestor[1]).astype(jnp.float32) - 2.0 * allele_freq.astype(jnp.float32) / 1000.0
    centered = lax.map(per_segment, jnp.arange(seg_total, dtype=jnp.int32))
    effects = jax.random.normal(jax.random.fold_in(key, 1000003), (P_SIZE, seg_total), jnp.float32) * jnp.sqrt(0.5 / (seg_total * 0.3))
    genetic = jnp.dot(effects, centered)
    noise_term = jax.random.normal(jax.random.fold_in(key, 1000004), (P_SIZE, NSAMP), jnp.float32) * 0.7071
    return jnp.clip(genetic + noise_term, -4.0, 4.0).astype(jnp.bfloat16)


def setup_inputs(seed: int = 0) -> dict:
    keys = jax.random.split(jax.random.key(seed), 4)
    genotypes = draw_genotypes(jax.random.fold_in(keys[3], 71), 0)
    phenotypes = draw_phenotypes(jax.random.fold_in(keys[3], 71), 0)
    trait_order = jax.random.permutation(keys[2], P_SIZE).astype(jnp.int32)
    return {"genotypes": genotypes, "phenotypes": phenotypes, "trait_order": trait_order}


LAMBDAS = (0.2, 2.0)
LEVEL_ONE = 0.1
EPSILON = 1e-06

def chebyshev(times_system, target, low_edge, high_edge):
    center = 0.5 * (high_edge + low_edge)
    radius = 0.5 * (high_edge - low_edge)
    sigma_ratio = center / radius
    rho_now = 1.0 / sigma_ratio
    direction = target / center
    solution = jnp.zeros_like(target)
    residual = target
    for iteration in range(ITERS):
        solution = solution + direction
        if iteration + 1 < ITERS:
            residual = residual - times_system(direction)
            rho_next = 1.0 / (2.0 * sigma_ratio - rho_now)
            direction = rho_next * rho_now * direction + 2.0 * rho_next / radius * residual
            rho_now = rho_next
    return solution

def reference(genotypes, phenotypes, trait_order):
    total_rows = S_DEV * N_FOLD
    held_rows = float(total_rows - S_DEV)
    penalty = jnp.array(LAMBDAS, jnp.float32)
    phen = jnp.take(phenotypes, trait_order, axis=0)
    phen_fold = phen.astype(jnp.float32).reshape(P_SIZE, N_FOLD, S_DEV)
    phen_sums = lax.optimization_barrier(jnp.sum(phen_fold, axis=2)).T
    phen_total = lax.optimization_barrier(jnp.sum(phen_sums, axis=0))
    geno = genotypes.reshape(N_FOLD, S_DEV, NB, B)

    def level_zero(block_index):
        block_dose = lax.dynamic_index_in_dim(geno, block_index, 2, False).astype(jnp.float32)
        gram_fold = jnp.einsum('ksi,ksj->kij', block_dose, block_dose)
        col_fold = lax.optimization_barrier(jnp.sum(block_dose, axis=1))
        cross_fold = jnp.einsum('pks,ksi->kpi', phen_fold, block_dose)
        gram_total = lax.optimization_barrier(jnp.sum(gram_fold, axis=0))
        col_total = lax.optimization_barrier(jnp.sum(col_fold, axis=0))
        cross_total = lax.optimization_barrier(jnp.sum(cross_fold, axis=0))
        mean_dose = col_total / total_rows
        inv_scale = 1.0 / jnp.sqrt(jnp.diagonal(gram_total) / total_rows - mean_dose * mean_dose + EPSILON)

        def one_fold(gram_own, col_own, cross_own, phen_own, dose_own):
            gram_out = gram_total - gram_own
            col_out = col_total - col_own
            cross_out = cross_total - cross_own
            phen_out = phen_total - phen_own
            centered = gram_out - col_out[:, None] * mean_dose[None, :] - mean_dose[:, None] * col_out[None, :] + held_rows * mean_dose[:, None] * mean_dose[None, :]
            system = inv_scale[:, None] * centered * inv_scale[None, :] / held_rows
            target = (cross_out - phen_out[:, None] * mean_dose[None, :]) * inv_scale[None, :] / held_rows
            bound = jnp.max(lax.optimization_barrier(jnp.sum(jnp.abs(system), axis=1)))
            low_edge = penalty[:, None, None]
            high_edge = low_edge + bound

            def times_system(direction):
                return jnp.einsum('rpi,ij->rpj', direction, system, precision=lax.Precision.HIGHEST) + low_edge * direction
            stacked = jnp.broadcast_to(target[None], (R,) + target.shape)
            coef = chebyshev(times_system, stacked, low_edge, high_edge)
            scaled = (inv_scale[None, None, :] * coef).astype(jnp.bfloat16)
            scaled_f32 = scaled.astype(jnp.float32)
            product = jnp.einsum('si,rpi->rps', dose_own, scaled_f32, precision=lax.Precision.HIGHEST)
            offset = jnp.einsum('i,rpi->rp', mean_dose, scaled_f32, precision=lax.Precision.HIGHEST)
            return (product - offset[:, :, None]).astype(jnp.bfloat16)
        return jax.vmap(one_fold)(gram_fold, col_fold, cross_fold, phen_sums, block_dose)
    feats = lax.map(level_zero, jnp.arange(NB, dtype=jnp.int32))
    feats = jnp.transpose(feats, (3, 1, 0, 2, 4)).reshape(P_SIZE, N_FOLD, Q, S_DEV)

    def level_one(operands):
        feat_trait, target_trait = operands
        feat_f32 = feat_trait.astype(jnp.float32)
        hgram_fold = jnp.einsum('kqs,kts->kqt', feat_f32, feat_f32)
        hcross_fold = jnp.einsum('kqs,ks->kq', feat_f32, target_trait)
        hgram_total = lax.optimization_barrier(jnp.sum(hgram_fold, axis=0))
        hcross_total = lax.optimization_barrier(jnp.sum(hcross_fold, axis=0))

        def solve_fold(hgram_own, hcross_own, feat_own):
            hgram_out = hgram_total - hgram_own
            hcross_out = hcross_total - hcross_own
            trace_sum = jnp.trace(hgram_out)
            level_system = hgram_out / held_rows + LEVEL_ONE * trace_sum / (held_rows * Q) * jnp.eye(Q, dtype=jnp.float32)
            factor = jnp.linalg.cholesky(level_system)
            weight = jax.scipy.linalg.cho_solve((factor, True), (hcross_out / held_rows)[:, None])[:, 0]
            return jnp.einsum('q,qs->s', weight, feat_own, precision=lax.Precision.HIGHEST)
        return jax.vmap(solve_fold)(hgram_fold, hcross_fold, feat_f32)
    predict = lax.map(level_one, (feats, phen_fold))
    return predict.reshape(P_SIZE, NSAMP)
```

```python
import functools

import jax
import jax.numpy as jnp
from jax import lax
from jax.experimental import pallas as pl
from jax.experimental.pallas import tpu as pltpu
from jax.sharding import PartitionSpec as P

B = 512
T = 128
ITERS = 8
LAMBDAS = (0.2, 2.0)
R = len(LAMBDAS)
LEVEL_ONE = 0.1
EPSILON = 1e-06
CHUNK = 1024
TILES = [(i, j) for i in range(B // T) for j in range(i, B // T)]
PACK = len(TILES) * T
HIGH = lax.Precision.HIGHEST
F32 = jnp.float32
BF16 = jnp.bfloat16
MESH = pl.DeviceIdType.MESH


def dot_nt(a, b):
    return lax.dot_general(a, b, (((1,), (1,)), ((), ())), preferred_element_type=F32)


def dot_nn(a, b, precision=None):
    return lax.dot_general(
        a, b, (((1,), (0,)), ((), ())), preferred_element_type=F32, precision=precision
    )


def iota(shape, axis):
    return lax.broadcasted_iota(jnp.int32, shape, axis)


def down(row):
    return jnp.transpose(jnp.broadcast_to(row, (T, row.shape[1])))


def kernel(
    n_f, n_b, order_ref, phen_ref, geno_ref, out_ref,
    xbuf, pa, gram, cross, gsend, grecv, gfull, csend, crecv, cfull, stats,
    s_hi, s_lo, fsend, frecv, hbuf,
    x_sem, gs_sem, gr_sem, cs_sem, cr_sem, ss_sem, sr_sem,
    g2s_sem, g2r_sem, c2s_sem, c2r_sem, fs_sem, fr_sem, fl_sem, hs_sem, hr_sem,
):
    rows = geno_ref.shape[0]
    blocks = geno_ref.shape[1] // B
    traits = phen_ref.shape[0]
    own = traits // n_b
    group = R * own
    q_total = n_b * blocks * R
    lanes = q_total * own
    g_rows = PACK // n_f
    c_rows = (B // T) * traits // n_f
    chunks = rows // CHUNK
    total_rows = float(rows * n_f)
    held = float(rows * (n_f - 1))
    me_f = lax.axis_index("fold")
    me_b = lax.axis_index("blk")

    def load(b, c):
        part = pl.ds(c * CHUNK, CHUNK)
        return pltpu.make_async_copy(
            geno_ref.at[part, pl.ds(b * B, B)], xbuf.at[b, part], x_sem.at[b, c]
        )

    for b in range(blocks):
        for c in range(chunks):
            load(b, c).start()

    fold_peers = [lax.rem(me_f + off, n_f) for off in range(1, n_f)]
    blk_peers = [lax.rem(me_b + off, n_b) for off in range(1, n_b)]
    barrier = pltpu.get_barrier_semaphore()
    for peer in fold_peers:
        pl.semaphore_signal(barrier, inc=1, device_id=(peer, me_b), device_id_type=MESH)
    for peer in blk_peers:
        pl.semaphore_signal(barrier, inc=1, device_id=(me_f, peer), device_id_type=MESH)

    pick = (iota((traits, traits), 0) == order_ref[...]).astype(F32).T.astype(BF16)
    pa[traits:, :] = jnp.ones((16, rows), BF16)

    @pl.loop(0, chunks)
    def _(c):
        part = pl.ds(pl.multiple_of(c * CHUNK, CHUNK), CHUNK)
        pa[:traits, part] = dot_nn(pick, phen_ref[:, part]).astype(BF16)

    psum_row = dot_nt(pa[traits:, :], pa[:traits, :])[:1, :]

    def fold_copy(src, dst, send, recv, peer):
        return pltpu.make_async_remote_copy(
            src_ref=src, dst_ref=dst, send_sem=send, recv_sem=recv,
            device_id=(peer, me_b), device_id_type=MESH,
        )

    pending = []
    first = [[] for _ in range(blocks)]
    small = [[] for _ in range(blocks)]
    second = [[] for _ in range(blocks)]

    for b in range(blocks):
        gram[...] = jnp.zeros_like(gram)
        cross[...] = jnp.zeros_like(cross)

        @pl.loop(0, chunks)
        def _(c, b=b):
            start = pl.multiple_of(c * CHUNK, CHUNK)
            load(b, c).wait()
            x = xbuf[b, pl.ds(start, CHUNK), :]
            xt = x.T
            half = B // 2
            gram[:half, :] += dot_nn(xt[:half], x)
            gram[half:, half:] += dot_nn(xt[half:], x[:, half:])
            cross[...] += dot_nn(pa[:, pl.ds(start, CHUNK)], x)

        col = cross[traits : traits + 1, :]
        col_down = down(col)
        mean_row = col * (1.0 / rows)
        diag = []
        eye = iota((T, T), 0) == iota((T, T), 1)
        for slot, (i, j) in enumerate(TILES):
            si, sj = slice(i * T, (i + 1) * T), slice(j * T, (j + 1) * T)
            tile = gram[si, sj] - col_down[si, :] * mean_row[:, sj]
            if i == j:
                diag.append(jnp.sum(jnp.where(eye, tile, 0.0), axis=0, keepdims=True))
            gsend[b, slot * T : (slot + 1) * T, :] = tile.astype(BF16)
        psum_down = jnp.transpose(jnp.broadcast_to(psum_row, (T, traits)))
        for i in range(B // T):
            si = slice(i * T, (i + 1) * T)
            csend[b, i * traits : (i + 1) * traits, :] = (
                cross[:traits, si] - psum_down * mean_row[:, si]
            )
        wide_psum = jnp.concatenate([psum_row, jnp.zeros((1, B - traits), F32)], axis=1)
        stats[b, me_f] = jnp.concatenate(
            [col, jnp.concatenate(diag, axis=1), wide_psum, jnp.zeros((5, B), F32)], axis=0
        )
        if b == 0:
            pl.semaphore_wait(barrier, n_f + n_b - 2)
        for k, peer in enumerate(fold_peers):
            sm = fold_copy(
                stats.at[b, me_f], stats.at[b, me_f], ss_sem.at[b, k], sr_sem.at[b, k], peer
            )
            gc = fold_copy(
                gsend.at[b, pl.ds(peer * g_rows, g_rows)], grecv.at[b, me_f],
                gs_sem.at[b, k], gr_sem.at[b, k], peer,
            )
            cc = fold_copy(
                csend.at[b, pl.ds(peer * c_rows, c_rows)], crecv.at[b, me_f],
                cs_sem.at[b, k], cr_sem.at[b, k], peer,
            )
            for copy in (sm, gc, cc):
                copy.start()
            small[b].append(sm)
            first[b] += [gc, cc]
            pending += [sm, gc, cc]

    for b in range(blocks):
        g_mine = pl.ds(me_f * g_rows, g_rows)
        c_mine = pl.ds(me_f * c_rows, c_rows)
        grecv[b, me_f] = gsend[b, g_mine, :]
        crecv[b, me_f] = csend[b, c_mine, :]
        for copy in first[b]:
            copy.wait_recv()
        g_sum = grecv[b, 0].astype(F32)
        c_sum = crecv[b, 0]
        for j in range(1, n_f):
            g_sum += grecv[b, j].astype(F32)
            c_sum += crecv[b, j]
        gfull[b, g_mine, :] = g_sum.astype(BF16)
        cfull[b, c_mine, :] = c_sum
        for k, peer in enumerate(fold_peers):
            gc = fold_copy(
                gfull.at[b, g_mine], gfull.at[b, g_mine], g2s_sem.at[b, k], g2r_sem.at[b, k], peer
            )
            cc = fold_copy(
                cfull.at[b, c_mine], cfull.at[b, c_mine], c2s_sem.at[b, k], c2r_sem.at[b, k], peer
            )
            gc.start()
            cc.start()
            second[b] += [gc, cc]
            pending += [gc, cc]

    feat_copies = []
    feat_local = []
    for b in range(blocks):
        for copy in small[b]:
            copy.wait_recv()
        cols = jnp.concatenate([stats[b, j, 0:1, :] for j in range(n_f)], axis=0)
        psums = jnp.concatenate([stats[b, j, 2:3, :] for j in range(n_f)], axis=0)
        within = stats[b, 0, 1:2, :]
        for j in range(1, n_f):
            within += stats[b, j, 1:2, :]
        mean = jnp.sum(cols, axis=0, keepdims=True) * (1.0 / total_rows)
        shift = cols * (1.0 / rows) - mean
        between = jnp.sum(shift * shift, axis=0, keepdims=True) * float(rows)
        inv = 1.0 / jnp.sqrt((within + between) * (1.0 / total_rows) + EPSILON)
        inv_down = down(inv)
        others = jnp.where(iota((n_f, B), 0) == me_f, 0.0, shift)
        others_t = jnp.transpose(others)
        psums_t = jnp.transpose(psums)[:traits, :]
        for copy in second[b]:
            copy.wait_recv()
        diag_out = within - stats[b, me_f, 1:2, :]
        eye = iota((T, T), 0) == iota((T, T), 1)
        reach = [jnp.zeros((1, T), F32) for _ in range(B // T)]
        for slot, (i, j) in enumerate(TILES):
            si, sj = slice(i * T, (i + 1) * T), slice(j * T, (j + 1) * T)
            sp = slice(slot * T, (slot + 1) * T)
            outer = dot_nn(others_t[si, :], others[:, sj], HIGH)
            tile = gfull[b, sp, :].astype(F32) - gsend[b, sp, :].astype(F32)
            if i == j:
                tile = jnp.where(eye, diag_out[:, sj], tile)
            tile = tile + float(rows) * outer
            tile = inv_down[si, :] * tile * (inv[:, sj] * (1.0 / held))
            reach[j] += jnp.sum(jnp.abs(tile), axis=0, keepdims=True)
            hi = tile.astype(BF16)
            s_hi[si, sj] = hi
            s_lo[si, sj] = (tile - hi.astype(F32)).astype(BF16)
            if i != j:
                tile = tile.T
                reach[i] += jnp.sum(jnp.abs(tile), axis=0, keepdims=True)
                hi = tile.astype(BF16)
                s_hi[sj, si] = hi
                s_lo[sj, si] = (tile - hi.astype(F32)).astype(BF16)
        bound = jnp.max(jnp.concatenate(reach, axis=1), axis=1, keepdims=True)
        moved = dot_nn(psums_t, others, HIGH)
        target = jnp.concatenate(
            [
                cfull[b, i * traits : (i + 1) * traits, :]
                - csend[b, i * traits : (i + 1) * traits, :]
                for i in range(B // T)
            ],
            axis=1,
        )
        target = (target + moved) * (inv * (1.0 / held))
        line = iota((R * traits, traits), 0)
        spread = iota((R * traits, traits), 1) == (line // group) * own + line % own
        target = dot_nn(spread.astype(F32), target, HIGH)
        low = jnp.where(
            (iota((R * traits, 1), 0) // own) % R == 0, F32(LAMBDAS[0]), F32(LAMBDAS[1])
        )
        high = low + bound
        center = 0.5 * (high + low)
        radius = 0.5 * (high - low)
        sigma = center / radius
        rho = 1.0 / sigma
        direction = target / center
        residual = target
        coef = jnp.zeros_like(target)
        for step in range(ITERS):
            coef = coef + direction
            if step + 1 < ITERS:
                d_hi = direction.astype(BF16)
                d_lo = (direction - d_hi.astype(F32)).astype(BF16)
                both = dot_nn(jnp.concatenate([d_hi, d_lo], axis=0), s_hi[...])
                times = both[: R * traits] + both[R * traits :] + dot_nn(d_hi, s_lo[...])
                residual = residual - (times + low * direction)
                rho_next = 1.0 / (2.0 * sigma - rho)
                direction = rho_next * rho * direction + 2.0 * rho_next / radius * residual
                rho = rho_next
        scaled = (coef * inv).astype(BF16)
        offset = jnp.sum(scaled.astype(F32) * mean, axis=1, keepdims=True)

        @pl.loop(0, chunks)
        def _(c, b=b, scaled=scaled, offset=offset):
            part = pl.ds(pl.multiple_of(c * CHUNK, CHUNK), CHUNK)
            feat = (dot_nt(scaled, xbuf[b, part, :]) - offset).astype(BF16)
            for d in range(n_b):
                fsend[b, d, :, part] = feat[d * group : (d + 1) * group, :]

        slot = me_b * blocks + b
        for k, peer in enumerate(blk_peers):
            copy = pltpu.make_async_remote_copy(
                src_ref=fsend.at[b, peer], dst_ref=frecv.at[slot],
                send_sem=fs_sem.at[b, k], recv_sem=fr_sem.at[b, k],
                device_id=(me_f, peer), device_id_type=MESH,
            )
            copy.start()
            feat_copies.append(copy)
            pending.append(copy)
        keep = pltpu.make_async_copy(fsend.at[b, me_b], frecv.at[slot], fl_sem.at[b])
        keep.start()
        feat_local.append(keep)

    for copy in feat_local:
        copy.wait()
    for copy in feat_copies:
        copy.wait_recv()

    def level(c):
        part = pl.ds(pl.multiple_of(c * CHUNK, CHUNK), CHUNK)
        return frecv[:, :, part].reshape(lanes, CHUNK), part

    def add_level(c, carry):
        hg, hc = carry
        feat, part = level(c)
        return hg + dot_nt(feat, feat), hc + dot_nt(pa[:traits, part], feat)

    hg, hc = lax.fori_loop(
        0, chunks, add_level, (jnp.zeros((lanes, lanes), F32), jnp.zeros((traits, lanes), F32))
    )
    same = iota((lanes, lanes), 0) % own == iota((lanes, lanes), 1) % own
    gather = (iota((q_total, lanes), 1) // own == iota((q_total, lanes), 0)).astype(F32)
    compact = dot_nn(gather, jnp.where(same, hg, 0.0), HIGH)
    mine = iota((traits, lanes), 0) == me_b * own + iota((traits, lanes), 1) % own
    right = jnp.sum(jnp.where(mine, hc, 0.0), axis=0, keepdims=True)
    hbuf[me_f, :q_total, :] = compact
    hbuf[me_f, q_total:, :] = jnp.broadcast_to(right, (8, lanes))
    h_copies = []
    for k, peer in enumerate(fold_peers):
        copy = fold_copy(hbuf.at[me_f], hbuf.at[me_f], hs_sem.at[k], hr_sem.at[k], peer)
        copy.start()
        h_copies.append(copy)
        pending.append(copy)
    for copy in h_copies:
        copy.wait_recv()
    hoo = jnp.zeros((q_total + 8, lanes), F32)
    for j in range(n_f):
        hoo += jnp.where(me_f == j, 0.0, hbuf[j])
    hoo = hoo * (1.0 / held)

    def all_groups(a):
        shift = own
        while shift < lanes:
            a = a + pltpu.roll(a, shift, 1)
            shift *= 2
        return a

    feature_of = iota((q_total, lanes), 1) // own
    on_diag = feature_of == iota((q_total, lanes), 0)
    system = hoo[:q_total]
    trace = jnp.sum(all_groups(jnp.where(on_diag, system, 0.0)), axis=0, keepdims=True)
    system = system + jnp.where(on_diag, (LEVEL_ONE / q_total) * trace, 0.0)
    rhs = all_groups(jnp.where(on_diag, hoo[q_total : q_total + 1], 0.0))
    for q in range(q_total):
        column = all_groups(jnp.where(feature_of == q, system, 0.0))
        inverse = 1.0 / column[q : q + 1]
        pivot = system[q : q + 1] * inverse
        pivot_rhs = rhs[q : q + 1] * inverse
        here = iota((q_total, lanes), 0) == q
        system = jnp.where(here, pivot, system - column * pivot)
        rhs = jnp.where(here, pivot_rhs, rhs - column * pivot_rhs)
    weight = jnp.sum(jnp.where(on_diag, rhs, 0.0), axis=0, keepdims=True)
    pad = 16
    weight = jnp.where(iota((pad, lanes), 1) % own == iota((pad, lanes), 0), weight, 0.0)
    w_hi = weight.astype(BF16)
    rest = weight - w_hi.astype(F32)
    w_mid = rest.astype(BF16)
    w_lo = (rest - w_mid.astype(F32)).astype(BF16)
    w_all = jnp.concatenate([w_hi, w_mid, w_lo], axis=0)

    @pl.loop(0, chunks)
    def _(c):
        feat, part = level(c)
        three = dot_nn(w_all, feat)
        out_ref[:, part] = (three[:pad] + three[pad : 2 * pad] + three[2 * pad :])[:own]

    for copy in pending:
        copy.wait_send()


def per_device(genotypes, phenotypes, trait_order):
    n_f = lax.axis_size("fold")
    n_b = lax.axis_size("blk")
    rows, variants = genotypes.shape
    blocks = variants // B
    traits = phenotypes.shape[0]
    own = traits // n_b
    q_total = n_b * blocks * R
    lanes = q_total * own
    c_all = (B // T) * traits
    dma = pltpu.SemaphoreType.DMA
    vmem = pltpu.VMEM
    return pl.pallas_call(
        functools.partial(kernel, n_f, n_b),
        out_shape=jax.ShapeDtypeStruct((own, rows), F32),
        in_specs=[
            pl.BlockSpec(memory_space=pltpu.VMEM),
            pl.BlockSpec(memory_space=pltpu.VMEM),
            pl.BlockSpec(memory_space=pl.ANY),
        ],
        out_specs=pl.BlockSpec(memory_space=pltpu.VMEM),
        scratch_shapes=[
            vmem((blocks, rows, B), BF16),
            vmem((traits + 16, rows), BF16),
            vmem((B, B), F32),
            vmem((traits + 16, B), F32),
            vmem((blocks, PACK, T), BF16),
            vmem((blocks, n_f, PACK // n_f, T), BF16),
            vmem((blocks, PACK, T), BF16),
            vmem((blocks, c_all, T), F32),
            vmem((blocks, n_f, c_all // n_f, T), F32),
            vmem((blocks, c_all, T), F32),
            vmem((blocks, n_f, 8, B), F32),
            vmem((B, B), BF16),
            vmem((B, B), BF16),
            vmem((blocks, n_b, R * own, rows), BF16),
            vmem((n_b * blocks, R * own, rows), BF16),
            vmem((n_f, q_total + 8, lanes), F32),
            dma((blocks, rows // CHUNK)),
        ]
        + [dma((blocks, n_f - 1)) for _ in range(10)]
        + [dma((blocks, n_b - 1)) for _ in range(2)]
        + [dma((blocks,))]
        + [dma((n_f - 1,)) for _ in range(2)],
        compiler_params=pltpu.CompilerParams(
            collective_id=0, has_side_effects=True, vmem_limit_bytes=52 * 1024 * 1024
        ),
    )(trait_order.reshape(1, traits), phenotypes, genotypes)


def solution(mesh):
    return jax.shard_map(
        per_device,
        mesh=mesh,
        in_specs=(P("fold", "blk"), P(None, "fold"), P()),
        out_specs=P("blk", "fold"),
        check_vma=False,
    )
```
